256 devices in a mesh: section: 64 (over x, z, y_hi), tp: 4 (over y_lo, core).
Axes of the slice: x: 4, y: 4 (y_hi: 2, y_lo: 2; y = y_hi * 2 + y_lo), z: 8, core: 2. Of those that a mesh axis runs over, the one named last changes fastest.
Arguments:
- query: bfloat16 [64, 2, 256, 4096], P('section', None, None, 'tp'), may hold values from -6 to 6
- keyval: bfloat16 [64, 768, 1024], P('section', None, 'tp'), may hold values from -6 to 6
- q_weight: bfloat16 [64, 4096, 4096], P('section', None, 'tp'), may hold values from -0.09375 to 0.09375
- kv_weight: bfloat16 [64, 4096, 1024], P('section', None, 'tp'), may hold values from -0.09375 to 0.09375
- block_index: int32 [64], P('section'), may hold values from 0 to 1
- carry_in: bfloat16 [64, 768, 1024], P('section', None, 'tp'), may hold values from -0.59765625 to 0.59765625
- grad_late: bfloat16 [64, 256, 4096], P('section', None, 'tp'), may hold values from -6 to 6
- grad_top: bfloat16 [256, 4096], P(None, 'tp'), may hold values from -6 to 6
Outputs:
- grad_early: bfloat16 [64, 256, 4096], P('section', None, 'tp')
- carry_out: bfloat16 [64, 768, 1024], P('section', None, 'tp')
The draws below stay inside these ranges and needn't reach their ends.
All inputs are finite; a program needn't handle non-finite values.
Results may differ from the reference program's by a relative error of at most 0.02.
Values may be sent and summed in bfloat16 or wider, within the bound.
No kernel may reach another device: no remote copies, remote signals or barrier semaphores. Data moves between devices by JAX's collectives and lax.ppermute only.
A program may use at most 64 MiB of HBM per device.

```python
import math
import jax
import jax.numpy as jnp
from jax import lax

D = 4096
HEADS = 32
KV_HEADS = 4
HD = 128
R = 256
NCHUNK = 3
SEQ = 768
SECTIONS = 64
N_TP = 4


def draw_query(key, part):
    key = jax.random.fold_in(key, 11)
    values = jnp.clip(jax.random.normal(key, (SECTIONS, 2, R, HEADS, HD), jnp.float32), -4.0, 4.0)
    return values.reshape(SECTIONS, 2, R, HEADS * HD).astype(jnp.bfloat16)


def draw_keyval(key, part):
    key = jax.random.fold_in(key, 23)
    values = jnp.clip(jax.random.normal(key, (SECTIONS, SEQ, KV_HEADS, 2, HD), jnp.float32), -4.0, 4.0)
    return values.reshape(SECTIONS, SEQ, KV_HEADS * 2 * HD).astype(jnp.bfloat16)


def touch_ends(values, own_key, least, top_value):
    longest = values.shape.index(max(values.shape))
    spots = []
    for shift in (0, 1):
        where = [jax.random.randint(jax.random.fold_in(own_key, axis), (), 0, length) for axis, length in enumerate(values.shape)]
        where[longest] = (where[longest] + shift) % values.shape[longest]
        spots.append(tuple(where))
    return values.at[spots[0]].set(least).at[spots[1]].set(top_value)


def shard_levels(stream_key, extent, split, smallest, top_value):
    def one(dim, shards_of):
        draws = jax.random.uniform(jax.random.fold_in(jax.random.fold_in(stream_key, 6), dim), (shards_of,), jnp.float32, smallest / len(split), top_value / len(split))
        return jnp.repeat(jnp.exp(draws), extent[dim] // shards_of).reshape((-1,) + (1,) * (len(extent) - dim - 1))

    level = one(*split[0])
    for cut in split[1:]:
        level = level * one(*cut)
    return level


def gaussian(key, extent, deviation, most, cuts=(), kind=jnp.bfloat16):
    drawn = deviation * jax.random.normal(key, extent, jnp.float32)
    if cuts:
        drawn = drawn * shard_levels(key, extent, cuts, -0.22, 0.18)
    return jnp.clip(drawn, -most, most).astype(kind)


def setup_inputs(seed: int = 0) -> dict:
    splits = jax.random.split(jax.random.key(seed), 9)
    query = draw_query(jax.random.fold_in(splits[8], 71), 0)
    keyval = draw_keyval(jax.random.fold_in(splits[8], 71), 0)
    q_weight = gaussian(splits[2], (SECTIONS, D, HEADS * HD), D ** -0.5, 0.09375, ((0, 64), (2, 4)))
    kv_weight = gaussian(splits[3], (SECTIONS, D, KV_HEADS * 2 * HD), D ** -0.5, 0.09375, ((0, 64), (2, 4)))
    block_index = touch_ends(jax.random.randint(splits[4], (SECTIONS,), 0, NCHUNK - 1), jax.random.fold_in(splits[4], 1), 0, (NCHUNK - 1) - 1).astype(jnp.int32)
    carry_in = gaussian(splits[5], (SECTIONS, SEQ, KV_HEADS * 2 * HD), 0.1, 0.59765625, ((0, 64), (2, 4)))
    grad_late = gaussian(splits[6], (SECTIONS, R, D), 1.0, 6.0, ((0, 64), (2, 4)))
    grad_top = gaussian(splits[7], (R, D), 1.0, 6.0, ((1, 4),))
    return dict(query=query, keyval=keyval, q_weight=q_weight, kv_weight=kv_weight, block_index=block_index, carry_in=carry_in, grad_late=grad_late, grad_top=grad_top)


def block_terms(queries, gradient, keyval, first_row):
    group_size = HEADS // KV_HEADS
    score_scale = 1.0 / math.sqrt(HD)
    q_heads = queries.astype(jnp.float32).reshape(R, KV_HEADS, group_size, HD)
    grad_heads = gradient.astype(jnp.float32).reshape(R, KV_HEADS, group_size, HD)
    kv_pairs = keyval.astype(jnp.float32).reshape(SEQ, KV_HEADS, 2, HD)
    key_rows = kv_pairs[:, :, 0]
    value_rows = kv_pairs[:, :, 1]
    scores = jnp.einsum('rgjd,tgd->grjt', q_heads, key_rows) * score_scale
    positions = first_row + jnp.arange(R, dtype=jnp.int32)
    visible = (jnp.arange(SEQ, dtype=jnp.int32)[None, :] <= positions[:, None])[None, :, None, :]
    masked = jnp.where(visible, scores, -1e+30)
    highest = lax.optimization_barrier(jnp.max(masked, axis=-1, keepdims=True))
    exponent = jnp.exp(masked - highest)
    attn_probs = exponent / lax.optimization_barrier(jnp.sum(exponent, axis=-1, keepdims=True))
    probs_low = lax.optimization_barrier(attn_probs.astype(jnp.bfloat16)).astype(jnp.float32)
    value_terms = jnp.einsum('grjt,rgjd->tgd', probs_low, grad_heads)
    grad_probs = jnp.einsum('rgjd,tgd->grjt', grad_heads, value_rows)
    row_delta = lax.optimization_barrier(jnp.sum(attn_probs * grad_probs, axis=-1, keepdims=True))
    grad_scores = lax.optimization_barrier((attn_probs * (grad_probs - row_delta)).astype(jnp.bfloat16)).astype(jnp.float32)
    grad_query = (jnp.einsum('grjt,tgd->rgjd', grad_scores, key_rows) * score_scale).astype(jnp.bfloat16)
    key_terms = jnp.einsum('grjt,rgjd->tgd', grad_scores, q_heads) * score_scale
    kv_terms = jnp.stack([key_terms, value_terms], axis=2).reshape(SEQ, KV_HEADS * 2 * HD)
    return (grad_query.reshape(R, HEADS * HD), kv_terms)

def project(grad_query, own_rows, q_local, kv_local):
    contract_dims = (((1,), (1,)), ((), ()))
    q_width = HEADS * HD // N_TP
    kv_width = KV_HEADS * 2 * HD // N_TP
    summed = jnp.zeros((R, D), jnp.float32)
    for group_index in range(N_TP):
        q_part = grad_query[:, group_index * q_width:(group_index + 1) * q_width]
        q_cols = q_local[:, group_index * q_width:(group_index + 1) * q_width]
        kv_part = own_rows[:, group_index * kv_width:(group_index + 1) * kv_width]
        kv_cols = kv_local[:, group_index * kv_width:(group_index + 1) * kv_width]
        partial_sum = lax.dot_general(q_part, q_cols, contract_dims, preferred_element_type=jnp.float32)
        partial_sum = partial_sum + lax.dot_general(kv_part, kv_cols, contract_dims, preferred_element_type=jnp.float32)
        summed = summed + lax.optimization_barrier(partial_sum.astype(jnp.bfloat16)).astype(jnp.float32)
    return summed

def late_tick(section_items):
    queries, keyval, q_local, kv_local, block_at, carried, gradient = section_items
    first_row = ((block_at + 1) * R).astype(jnp.int32)
    grad_query, kv_terms = block_terms(queries, gradient, keyval, first_row)
    running = carried.astype(jnp.float32) + kv_terms
    own_rows = lax.dynamic_slice_in_dim(running, first_row, R, 0).astype(jnp.bfloat16)
    late_dx = (gradient.astype(jnp.float32) + project(grad_query, own_rows, q_local, kv_local)).astype(jnp.bfloat16)
    return (late_dx, running)

def early_tick(section_items):
    queries, keyval, q_local, kv_local, block_at, running, gradient = section_items
    first_row = (block_at * R).astype(jnp.int32)
    grad_query, kv_terms = block_terms(queries, gradient, keyval, first_row)
    running_next = running + kv_terms
    own_rows = lax.dynamic_slice_in_dim(running_next, first_row, R, 0).astype(jnp.bfloat16)
    early_dx = (gradient.astype(jnp.float32) + project(grad_query, own_rows, q_local, kv_local)).astype(jnp.bfloat16)
    below = jnp.arange(SEQ, dtype=jnp.int32)[:, None] < first_row
    carried_out = jnp.where(below, running_next, jnp.zeros_like(running_next)).astype(jnp.bfloat16)
    return (early_dx, carried_out)

def reference(query, keyval, q_weight, kv_weight, block_index, carry_in, grad_late, grad_top):
    late_out, runnings = lax.map(late_tick, (query[:, 0], keyval, q_weight, kv_weight, block_index, carry_in, grad_late))
    early_in = jnp.concatenate([late_out[1:], grad_top[None]], axis=0)
    grad_early, carry_out = lax.map(early_tick, (query[:, 1], keyval, q_weight, kv_weight, block_index, runnings, early_in))
    return (grad_early, carry_out)
```

```python
import functools
import math

import jax
import jax.numpy as jnp
from jax import lax
from jax.experimental import pallas as pl
from jax.experimental.pallas import tpu as pltpu
from jax.sharding import PartitionSpec as P

HD = 128
BLOCK = 256
WIDTH = 1024
KV_WIDTH = 256
CHUNKS = ((128, 256), (0, 128))
NT = (((1,), (1,)), ((), ()))
NN = (((1,), (0,)), ((), ()))


def dot(a, b, dims=NN):
    return lax.dot_general(a, b, dims, preferred_element_type=jnp.float32)


def attend(q, do, kv_ref, visible_to, keys, dq_ref, pairs, running):
    rows = q.shape[0]
    heads = q.shape[1] // HD
    scale = 1.0 / math.sqrt(HD)
    key_rows = kv_ref[:keys, :HD]
    value_rows = kv_ref[:keys, HD:]
    keys_t = key_rows.astype(jnp.float32).T.astype(jnp.bfloat16)
    lane = lax.broadcasted_iota(jnp.int32, (keys, pairs * rows), 1)
    position = visible_to + lax.rem(lane, rows)
    key_at = lax.broadcasted_iota(jnp.int32, (keys, pairs * rows), 0)
    bias = jnp.where(key_at <= position, 0.0, -1e30)
    dk = jnp.zeros((keys, HD), jnp.float32)
    dv = jnp.zeros((keys, HD), jnp.float32)
    for base in range(0, heads, pairs):
        cols = [slice((base + j) * HD, (base + j + 1) * HD) for j in range(pairs)]
        q_g = jnp.concatenate([q[:, c] for c in cols], axis=0)
        do_g = jnp.concatenate([do[:, c] for c in cols], axis=0)
        s = dot(key_rows, q_g, NT) * (scale * math.log2(math.e)) + bias
        e = jnp.exp2(s - jnp.max(s, axis=0, keepdims=True))
        p = e * (1.0 / jnp.sum(e, axis=0, keepdims=True))
        dv = dv + dot(p.astype(jnp.bfloat16), do_g)
        dp = dot(value_rows, do_g, NT)
        delta = jnp.sum(p * dp, axis=0, keepdims=True)
        ds = (p * (dp - delta)).astype(jnp.bfloat16)
        dk = dk + dot(ds, q_g)
        dq = (dot(keys_t, ds) * scale).T.astype(jnp.bfloat16)
        for j, c in enumerate(cols):
            dq_ref[:, c] = dq[j * rows : (j + 1) * rows]
    running[:keys, :HD] += dk * scale
    running[:keys, HD:] += dv


def stage(early, lo, hi, first, last, *refs):
    refs = list(refs)
    block_ref, q_ref, do_ref = refs[:3]
    del refs[:3]
    if early:
        top_ref, flag_ref = refs[:2]
        del refs[:2]
    kv_ref, run_in, wq_hbm, wkv_hbm = refs[:4]
    del refs[:4]
    part_out = refs.pop(0)
    run_out = refs.pop(0)
    wq, wkv, running, carry, dq_ref, part, w_sem, part_sem, run_sem = refs
    tp = lax.axis_index("tp")
    shards = [tp ^ 1, tp, tp ^ 3, tp ^ 2] if not early else [tp ^ 3, tp ^ 2, tp ^ 1, tp]
    own_slot = 1 if not early else 3
    rows = hi - lo
    copies = []
    for i, shard in enumerate(shards):
        at = pl.ds(pl.multiple_of(shard * WIDTH, WIDTH), WIDTH)
        copies.append(
            (
                pltpu.make_async_copy(wq_hbm.at[0, at], wq.at[i], w_sem.at[i, 0]),
                pltpu.make_async_copy(wkv_hbm.at[0, at], wkv.at[i], w_sem.at[i, 1]),
            )
        )
    if first:
        run_copy = pltpu.make_async_copy(run_in.at[0], carry, run_sem.at[0])
    else:
        run_copy = pltpu.make_async_copy(run_in, running, run_sem.at[0])
    run_copy.start()
    for pair in copies:
        for copy in pair:
            copy.start()
    block = block_ref[0] + (0 if early else 1)
    first_row = block * BLOCK
    keys = (BLOCK if early else 2 * BLOCK) + hi
    q = q_ref[0, 0]
    if early:
        do = jnp.where(flag_ref[0] == 1, top_ref[...], do_ref[...])
    else:
        do = do_ref[0]
    run_copy.wait()
    if first:
        running[...] = carry[...].astype(jnp.float32)
    attend(q, do, kv_ref.at[0], first_row + lo, keys, dq_ref, BLOCK // rows, running)
    if last:
        below = lax.broadcasted_iota(jnp.int32, running.shape, 0) < first_row
        carry[...] = jnp.where(below, running[...], 0.0).astype(jnp.bfloat16)
        out_copy = pltpu.make_async_copy(carry, run_out.at[0], run_sem.at[1])
    else:
        out_copy = pltpu.make_async_copy(running, run_out, run_sem.at[1])
    out_copy.start()
    own = running[pl.ds(pl.multiple_of(first_row + lo, 64), rows), :].astype(jnp.bfloat16)
    dq = dq_ref[...]
    outs = []
    for i in range(4):
        for copy in copies[i]:
            copy.wait()
        total = dot(dq, wq[i], NT) + dot(own, wkv[i], NT)
        if i == own_slot:
            total = total + do.astype(jnp.float32)
        part[i] = total.astype(jnp.bfloat16)
        copy = pltpu.make_async_copy(part.at[i], part_out.at[i], part_sem.at[i])
        copy.start()
        outs.append(copy)
    for copy in outs:
        copy.wait()
    out_copy.wait()


def run_stage(early, lo, hi, first, last, block, query, do, top, flag, keyval, run, wq, wkv):
    rows = hi - lo
    row_block = lo // rows
    smem = pl.BlockSpec(memory_space=pltpu.SMEM)
    hbm = pl.BlockSpec(memory_space=pl.ANY)
    length = keyval.shape[1]
    in_specs = [
        smem,
        pl.BlockSpec((1, 1, rows, WIDTH), lambda i: (0, 1 if early else 0, row_block, 0)),
    ]
    args = [block, query, do]
    if early:
        in_specs += [
            pl.BlockSpec((rows, WIDTH), lambda i: (0, 0)),
            pl.BlockSpec((rows, WIDTH), lambda i: (row_block, 0)),
            smem,
        ]
        args += [top, flag]
    else:
        in_specs += [pl.BlockSpec((1, rows, WIDTH), lambda i: (0, row_block, 0))]
    in_specs += [
        pl.BlockSpec((1, length, KV_WIDTH), lambda i: (0, 0, 0)),
        hbm,
        hbm,
        hbm,
    ]
    args += [keyval, run, wq, wkv]
    if last:
        run_shape = jax.ShapeDtypeStruct((1, length, KV_WIDTH), jnp.bfloat16)
    else:
        run_shape = jax.ShapeDtypeStruct((length, KV_WIDTH), jnp.float32)
    return pl.pallas_call(
        functools.partial(stage, early, lo, hi, first, last),
        grid=(1,),
        out_shape=(jax.ShapeDtypeStruct((4, rows, WIDTH), jnp.bfloat16), run_shape),
        in_specs=in_specs,
        out_specs=(hbm, hbm),
        scratch_shapes=[
            pltpu.VMEM((4, WIDTH, WIDTH), jnp.bfloat16),
            pltpu.VMEM((4, WIDTH, KV_WIDTH), jnp.bfloat16),
            pltpu.VMEM((length, KV_WIDTH), jnp.float32),
            pltpu.VMEM((length, KV_WIDTH), jnp.bfloat16),
            pltpu.VMEM((rows, WIDTH), jnp.bfloat16),
            pltpu.VMEM((4, rows, WIDTH), jnp.bfloat16),
            pltpu.SemaphoreType.DMA((4, 2)),
            pltpu.SemaphoreType.DMA((4,)),
            pltpu.SemaphoreType.DMA((2,)),
        ],
        compiler_params=pltpu.CompilerParams(vmem_limit_bytes=48 * 1024 * 1024),
        cost_estimate=pl.CostEstimate(
            flops=2 * rows * 1280 * 4096 + 20 * 8 * rows * 640 * HD,
            bytes_accessed=13 * 1024 * 1024,
            transcendentals=0,
        ),
        name=("early" if early else "late") + str(lo),
    )(*args)


def swap(block, mask):
    return lax.ppermute(block, "tp", [(i, i ^ mask) for i in range(lax.axis_size("tp"))])


def shift_down(block):
    sections, tp = lax.axis_size("section"), lax.axis_size("tp")
    route = [
        (s * tp + t, (s - 1) * tp + (t ^ 2)) for s in range(1, sections) for t in range(tp)
    ]
    return lax.ppermute(block, ("section", "tp"), route)


def total_of(*terms):
    out = terms[0].astype(jnp.float32)
    for term in terms[1:]:
        out = out + term.astype(jnp.float32)
    return out.astype(jnp.bfloat16)


def local(query, keyval, q_weight, kv_weight, block_index, carry_in, grad_late, grad_top):
    run = carry_in
    shifted = []
    for n, (lo, hi) in enumerate(CHUNKS):
        part, run = run_stage(
            False, lo, hi, n == 0, False, block_index, query, grad_late, None, None,
            keyval, run, q_weight, kv_weight,
        )
        ahead = total_of(part[1], swap(part[0], 1))
        rest = (part[3], swap(part[2], 1))
        shifted.append(shift_down(total_of(*rest, swap(ahead, 2))))
    is_last = lax.axis_index("section") == lax.axis_size("section") - 1
    flag = is_last.astype(jnp.int32).reshape(1)
    outs = {}
    for n, (lo, hi) in enumerate(CHUNKS):
        last = n == len(CHUNKS) - 1
        part, run = run_stage(
            True, lo, hi, False, last, block_index, query, shifted[n], grad_top, flag,
            keyval, run, q_weight, kv_weight,
        )
        ahead = total_of(part[1], swap(part[0], 1))
        rest = (part[3], swap(part[2], 1))
        outs[lo] = total_of(*rest, swap(ahead, 2))
    early_dx = jnp.concatenate([outs[lo] for lo in sorted(outs)], axis=0)
    return (early_dx[None], run)


def solution(mesh):
    in_specs = (
        P("section", None, None, "tp"),
        P("section", None, "tp"),
        P("section", None, "tp"),
        P("section", None, "tp"),
        P("section"),
        P("section", None, "tp"),
        P("section", None, "tp"),
        P(None, "tp"),
    )
    out_specs = (P("section", None, "tp"), P("section", None, "tp"))
    return jax.shard_map(local, mesh=mesh, in_specs=in_specs, out_specs=out_specs, check_vma=False)
```

```python
import functools
import math

import jax
import jax.numpy as jnp
from jax import lax
from jax.experimental import pallas as pl
from jax.experimental.pallas import tpu as pltpu
from jax.sharding import PartitionSpec as P

HD = 128
BLOCK = 256
WIDTH = 1024
KV_WIDTH = 256
HALVES = ((128, 256), (0, 128))
PIECES = 4
NT = (((1,), (1,)), ((), ()))
NN = (((1,), (0,)), ((), ()))


def dot(a, b, dims=NN):
    return lax.dot_general(a, b, dims, preferred_element_type=jnp.float32)


def tall(ref, rows_at, out):
    heads = ref.shape[-1] // HD
    rows = rows_at.stop - rows_at.start
    for h in range(heads):
        out[h * rows : (h + 1) * rows] = ref[rows_at, h * HD : (h + 1) * HD]


def probabilities(key_rows, q_g, bias):
    scale = math.log2(math.e) / math.sqrt(HD)
    s = dot(key_rows, q_g, NT) * scale + bias
    e = jnp.exp2(s - jnp.max(s, axis=0, keepdims=True))
    return e * (1.0 / jnp.sum(e, axis=0, keepdims=True))


def visible_bias(keys, first_row, rows, lanes):
    position = first_row + lax.rem(lax.broadcasted_iota(jnp.int32, (keys, lanes), 1), rows)
    key_at = lax.broadcasted_iota(jnp.int32, (keys, lanes), 0)
    return jnp.where(key_at <= position, 0.0, -1e30)


def grad_scores(p, dp):
    delta = jnp.sum(p * dp, axis=0, keepdims=True)
    return (p * (dp - delta)).astype(jnp.bfloat16)


def add_terms(keys, kv_ref, q_all, do_all, p_all, ds_all, running, dq_ref, dq_rows):
    rows = dq_rows.stop - dq_rows.start
    scale = 1.0 / math.sqrt(HD)
    ds = ds_all[:keys]
    running[:keys, :HD] += dot(ds, q_all[...]) * scale
    running[:keys, HD:] += dot(p_all[:keys], do_all[...])
    keys_t = kv_ref[:keys, :HD].astype(jnp.float32).T.astype(jnp.bfloat16)
    dq = dot(keys_t, ds) * scale
    for h in range(dq.shape[1] // rows):
        piece = dq[:, h * rows : (h + 1) * rows].T
        dq_ref[dq_rows, h * HD : (h + 1) * HD] = piece.astype(jnp.bfloat16)


def start_all(copies):
    for copy in copies:
        copy.start()


def wait_all(copies):
    for copy in copies:
        copy.wait()


def project(dq, own, wq, wkv, slot):
    return dot(dq, wq[slot], NT) + dot(own, wkv[slot], NT)


def late_first(
    block_ref, q_hbm, do_hbm, kv_hbm, carry_hbm, wq_hbm, wkv_hbm,
    send_ref, keep_ref, run_hbm, dq_ref, own_ref, wq, wkv,
    run_ref, kv_ref, carry, q_ref, do_ref, q_all, do_all, p_all, ds_all, sem, w_sem,
):
    tp = lax.axis_index("tp")
    copies = [
        pltpu.make_async_copy(q_hbm.at[0, 0], q_ref, sem.at[0]),
        pltpu.make_async_copy(kv_hbm.at[0], kv_ref, sem.at[1]),
        pltpu.make_async_copy(do_hbm.at[0], do_ref, sem.at[2]),
        pltpu.make_async_copy(carry_hbm.at[0], carry, sem.at[3]),
    ]
    loads = []
    for i, shard in enumerate((tp ^ 1, tp, tp ^ 3, tp ^ 2)):
        at = pl.ds(pl.multiple_of(shard * WIDTH, WIDTH), WIDTH)
        loads.append(pltpu.make_async_copy(wq_hbm.at[0, at], wq.at[i], w_sem.at[i, 0]))
        loads.append(pltpu.make_async_copy(wkv_hbm.at[0, at], wkv.at[i], w_sem.at[i, 1]))
    start_all(copies)
    wait_all(copies)
    start_all(loads)
    first_row = (block_ref[0] + 1) * BLOCK
    keys = 3 * BLOCK
    tall(q_ref, slice(0, BLOCK), q_all)
    tall(do_ref, slice(0, BLOCK), do_all)
    run_ref[...] = carry[...].astype(jnp.float32)
    bias = visible_bias(keys, first_row, BLOCK, BLOCK)
    for h in range(WIDTH // HD):
        at = slice(h * BLOCK, (h + 1) * BLOCK)
        p = probabilities(kv_ref[:, :HD], q_all[at], bias)
        p_all[:, at] = p.astype(jnp.bfloat16)
        ds_all[:, at] = grad_scores(p, dot(kv_ref[:, HD:], do_all[at], NT))
    add_terms(
        keys, kv_ref, q_all, do_all, p_all, ds_all, run_ref, dq_ref, slice(0, BLOCK)
    )
    run_copy = pltpu.make_async_copy(run_ref, run_hbm, sem.at[4])
    run_copy.start()
    own_ref[...] = run_ref[pl.ds(pl.multiple_of(first_row, BLOCK), BLOCK), :].astype(jnp.bfloat16)
    wait_all(loads)
    dq, own = dq_ref[...], own_ref[...]
    send_ref[...] = project(dq, own, wq, wkv, 0).astype(jnp.bfloat16)
    keep = project(dq, own, wq, wkv, 1) + do_ref[...].astype(jnp.float32)
    keep_ref[...] = keep.astype(jnp.bfloat16)
    run_copy.wait()


def late_second(dq_ref, own_ref, wq, wkv, send_ref, keep_ref):
    dq, own = dq_ref[...], own_ref[...]
    send_ref[...] = project(dq, own, wq, wkv, 2).astype(jnp.bfloat16)
    keep_ref[...] = project(dq, own, wq, wkv, 3).astype(jnp.bfloat16)


def early_probabilities(
    block_ref, q_hbm, kv_hbm, p_b_hbm, p_t_hbm, p_b, p_t, q_all, kv_ref, q_ref, sem, p_sem
):
    copies = [
        pltpu.make_async_copy(q_hbm.at[0, 1], q_ref, sem.at[0]),
        pltpu.make_async_copy(kv_hbm.at[0], kv_ref, sem.at[1]),
    ]
    start_all(copies)
    wait_all(copies)
    outs = []
    for n, ((lo, hi), p_ref, out) in enumerate(zip(HALVES, (p_b, p_t), (p_b_hbm, p_t_hbm))):
        rows = hi - lo
        keys = BLOCK + hi
        tall(q_ref, slice(lo, hi), q_all)
        bias = visible_bias(keys, block_ref[0] * BLOCK + lo, rows, 2 * rows)
        for base in range(0, q_all.shape[0], 2 * rows):
            at = slice(base, base + 2 * rows)
            p = probabilities(kv_ref[:keys, :HD], q_all[at], bias)
            p_ref[:, at] = p.astype(jnp.bfloat16)
        outs.append(pltpu.make_async_copy(p_ref, out, p_sem.at[n]))
        outs[n].start()
    wait_all(outs)


def early_terms(lo, hi, flag_ref, passed, top_ref, kv_ref, q_all, p_ref, run_ref,
                do_ref, do_all, ds_all, dq_ref):
    rows = hi - lo
    keys = BLOCK + hi
    do_ref[lo:hi] = jnp.where(flag_ref[0] == 1, top_ref[...], passed)
    tall(do_ref, slice(lo, hi), do_all)
    for base in range(0, do_all.shape[0], 2 * rows):
        at = slice(base, base + 2 * rows)
        p = p_ref[:, at].astype(jnp.float32)
        ds_all[:keys, at] = grad_scores(p, dot(kv_ref[:keys, HD:], do_all[at], NT))
    add_terms(keys, kv_ref, q_all, do_all, p_ref, ds_all, run_ref, dq_ref, slice(lo, hi))


def early_top(
    flag_ref, do_in, do_more, q_hbm, top_hbm, kv_hbm, p_t_hbm, p_b_hbm, run_hbm,
    run_ref, dq_ref, do_out, kv_ref, p_b, qall_b, top_b,
    q_ref, top_ref, p_ref, q_all, do_ref, do_all, ds_all, dq_all, sem,
):
    (lo_b, hi_b), (lo, hi) = HALVES
    first = [
        pltpu.make_async_copy(top_hbm.at[lo:hi], top_ref, sem.at[0]),
        pltpu.make_async_copy(kv_hbm.at[0], kv_ref, sem.at[1]),
        pltpu.make_async_copy(p_t_hbm, p_ref, sem.at[2]),
    ]
    then = [
        pltpu.make_async_copy(q_hbm.at[0, 1], q_ref, sem.at[3]),
        pltpu.make_async_copy(run_hbm, run_ref, sem.at[4]),
    ]
    later = [
        pltpu.make_async_copy(p_b_hbm, p_b, sem.at[5]),
        pltpu.make_async_copy(top_hbm.at[lo_b:hi_b], top_b, sem.at[6]),
    ]
    start_all(first)
    start_all(then)
    passed = do_in[...].astype(jnp.float32) + do_more[...].astype(jnp.float32)
    wait_all(first)
    wait_all(then)
    start_all(later)
    tall(q_ref, slice(lo, hi), q_all)
    tall(q_ref, slice(lo_b, hi_b), qall_b)
    early_terms(lo, hi, flag_ref, passed.astype(jnp.bfloat16), top_ref, kv_ref, q_all, p_ref,
                run_ref, do_ref, do_all, ds_all, dq_all)
    dq_ref[...] = dq_all[lo:hi]
    do_out[...] = do_ref[lo:hi]
    wait_all(later)


def early_bottom(
    block_ref, flag_ref, do_in, top_ref, kv_ref, q_all, p_ref, run_in, dq_in, do_t,
    wq_hbm, wkv_hbm,
    send_ref, keep_ref, carry_ref, dq_ref, own_ref, do_ref, wq_out, wkv_out,
    wq, wkv, running, do_all, ds_all, w_sem,
):
    tp = lax.axis_index("tp")
    loads = []
    for i, shard in enumerate((tp ^ 3, tp ^ 2, tp ^ 1, tp)):
        at = pl.ds(pl.multiple_of(shard * WIDTH, WIDTH), WIDTH)
        q_to, kv_to = (wq.at[i], wkv.at[i]) if i < 2 else (wq_out.at[i - 2], wkv_out.at[i - 2])
        loads.append(pltpu.make_async_copy(wq_hbm.at[0, at], q_to, w_sem.at[i, 0]))
        loads.append(pltpu.make_async_copy(wkv_hbm.at[0, at], kv_to, w_sem.at[i, 1]))
    start_all(loads)
    lo, hi = HALVES[0]
    running[...] = run_in[...]
    dq_ref[:lo] = dq_in[...]
    do_ref[:lo] = do_t[...]
    early_terms(lo, hi, flag_ref, do_in[...], top_ref, kv_ref, q_all, p_ref, running,
                do_ref, do_all, ds_all, dq_ref)
    first_row = block_ref[0] * BLOCK
    own_ref[...] = running[pl.ds(pl.multiple_of(first_row, BLOCK), BLOCK), :].astype(jnp.bfloat16)
    below = lax.broadcasted_iota(jnp.int32, running.shape, 0) < first_row
    carry_ref[0] = jnp.where(below, running[...], 0.0).astype(jnp.bfloat16)
    dq, own = dq_ref[...], own_ref[...]
    wait_all(loads[:2])
    send_ref[...] = project(dq, own, wq, wkv, 0).astype(jnp.bfloat16)
    wait_all(loads[2:4])
    keep_ref[...] = project(dq, own, wq, wkv, 1).astype(jnp.bfloat16)
    wait_all(loads[4:])


def add_rows(*refs):
    *ins, out_ref = refs
    out_ref[...] = total_of(*(ref[...] for ref in ins))


def add_halves(a_ref, b_ref, top_ref, bottom_ref):
    half = top_ref.shape[0]
    top_ref[...] = total_of(a_ref[:half], b_ref[:half])
    bottom_ref[...] = total_of(a_ref[half:], b_ref[half:])


def early_second(dq_ref, own_ref, do_ref, wq, wkv, send_ref, keep_ref):
    dq, own = dq_ref[...], own_ref[...]
    send_ref[...] = project(dq, own, wq, wkv, 0).astype(jnp.bfloat16)
    keep = project(dq, own, wq, wkv, 1) + do_ref[...].astype(jnp.float32)
    keep_ref[...] = keep.astype(jnp.bfloat16)


def finish(keep_ref, got_ref, *refs):
    *pieces, out_ref = refs
    rows = pieces[0].shape[0]
    for i, piece in enumerate(pieces):
        at = slice(i * rows, (i + 1) * rows)
        out_ref[0, at] = total_of(keep_ref[at], got_ref[at], piece[...])


SMEM = pl.BlockSpec(memory_space=pltpu.SMEM)
HBM = pl.BlockSpec(memory_space=pltpu.HBM)
VMEM = pl.BlockSpec(memory_space=pltpu.VMEM)


def call(kernel, name, specs, args, outs, scratch, megabytes):
    args = [
        pltpu.with_memory_space_constraint(arg, pltpu.HBM) if spec is HBM else arg
        for arg, spec in zip(args, specs)
    ]
    return pl.pallas_call(
        kernel,
        out_shape=[
            pltpu.HBM(*out[:2]) if len(out) > 2 else jax.ShapeDtypeStruct(*out) for out in outs
        ],
        in_specs=specs,
        out_specs=[HBM if len(out) > 2 else VMEM for out in outs],
        scratch_shapes=scratch,
        compiler_params=pltpu.CompilerParams(vmem_limit_bytes=megabytes * 1024 * 1024),
        cost_estimate=pl.CostEstimate(
            flops=2 * 10**9, bytes_accessed=10**6, transcendentals=0
        ),
        name=name,
    )(*args)


def add(name, *terms):
    shape = terms[0].shape
    (out,) = call(
        add_rows, name, [VMEM] * len(terms), terms, [(shape, jnp.bfloat16)], [], 4
    )
    return out


def swap(block, mask):
    return lax.ppermute(block, "tp", [(i, i ^ mask) for i in range(lax.axis_size("tp"))])


def shift_down(block, mask):
    sections, tp = lax.axis_size("section"), lax.axis_size("tp")
    route = [
        (s * tp + t, (s - 1) % sections * tp + (t ^ mask))
        for s in range(sections)
        for t in range(tp)
    ]
    return lax.ppermute(block, ("section", "tp"), route)


def total_of(*terms):
    out = terms[0].astype(jnp.float32)
    for term in terms[1:]:
        out = out + term.astype(jnp.float32)
    return out.astype(jnp.bfloat16)


def local(query, keyval, q_weight, kv_weight, block_index, carry_in, grad_late, grad_top):
    is_last = lax.axis_index("section") == lax.axis_size("section") - 1
    flag = is_last.astype(jnp.int32).reshape(1)
    length = keyval.shape[1]
    half = BLOCK // 2
    tall_rows = BLOCK * WIDTH // HD
    bf16, f32 = jnp.bfloat16, jnp.float32
    block = ((BLOCK, WIDTH), bf16)
    half_block = ((half, WIDTH), bf16)
    half_tall = ((tall_rows // 2, HD), bf16)
    own_rows = ((BLOCK, KV_WIDTH), bf16)
    run_shape = ((length, KV_WIDTH), f32)
    kv_shape = ((length, KV_WIDTH), bf16)
    p_shapes = [((BLOCK + hi, tall_rows // 2), bf16) for _, hi in HALVES]
    q_load, kv_load = ((WIDTH, WIDTH), bf16), ((WIDTH, KV_WIDTH), bf16)
    several = lambda n, shape: ((n, *shape[0]), shape[1])
    send, keep, run, dq, own, wq, wkv = call(
        late_first,
        "late_first",
        [SMEM] + [HBM] * 6,
        [block_index, query, grad_late, keyval, carry_in, q_weight, kv_weight],
        [block, block, (*run_shape, HBM), block, own_rows]
        + [several(4, q_load), several(4, kv_load)],
        [
            pltpu.VMEM(*run_shape),
            pltpu.VMEM(*kv_shape),
            pltpu.VMEM(*kv_shape),
            pltpu.VMEM(*block),
            pltpu.VMEM(*block),
            pltpu.VMEM((tall_rows, HD), bf16),
            pltpu.VMEM((tall_rows, HD), bf16),
            pltpu.VMEM((length, tall_rows), bf16),
            pltpu.VMEM((length, tall_rows), bf16),
            pltpu.SemaphoreType.DMA((5,)),
            pltpu.SemaphoreType.DMA((4, 2)),
        ],
        20,
    )
    got = swap(send, 1)
    send2, keep2 = call(
        late_second, "late_second", [VMEM] * 4, [dq, own, wq, wkv], [block] * 2, [], 8
    )
    got2 = swap(send2, 1)
    mine_t, mine_b = call(
        add_halves, "add_mine", [VMEM] * 2, [keep, got], [half_block] * 2, [], 4
    )
    straight = shift_down(mine_t, 0)
    other = swap(mine_b, 2)
    crossed, kept = call(
        add_halves, "add_crossed", [VMEM] * 2, [keep2, got2], [half_block, half_block], [], 4
    )
    crossed = shift_down(crossed, 2)
    summed = shift_down(add("add_summed", kept, other), 2)
    p_b, p_t = call(
        early_probabilities,
        "early_probabilities",
        [SMEM, HBM, HBM],
        [block_index, query, keyval],
        [(*shape, HBM) for shape in p_shapes],
        [pltpu.VMEM(*shape) for shape in p_shapes]
        + [
            pltpu.VMEM(*half_tall),
            pltpu.VMEM(*kv_shape),
            pltpu.VMEM(*block),
            pltpu.SemaphoreType.DMA((2,)),
            pltpu.SemaphoreType.DMA((2,)),
        ],
        10,
    )
    run, dq_t, do_t, kv_held, p_b, qall_b, top_b = call(
        early_top,
        "early_top",
        [SMEM, VMEM, VMEM] + [HBM] * 6,
        [flag, straight, crossed, query, grad_top, keyval, p_t, p_b, run],
        [run_shape, half_block, half_block, kv_shape, p_shapes[0], half_tall, half_block],
        [
            pltpu.VMEM(*block),
            pltpu.VMEM(*half_block),
            pltpu.VMEM(*p_shapes[1]),
            pltpu.VMEM(*half_tall),
            pltpu.VMEM(*block),
            pltpu.VMEM(*half_tall),
            pltpu.VMEM(*p_shapes[0]),
            pltpu.VMEM(*block),
            pltpu.SemaphoreType.DMA((7,)),
        ],
        16,
    )
    send, keep, carry, dq, own, do, wq, wkv = call(
        early_bottom,
        "early_bottom",
        [SMEM, SMEM] + [VMEM] * 8 + [HBM] * 2,
        [block_index, flag, summed, top_b, kv_held, qall_b, p_b, run, dq_t, do_t]
        + [q_weight, kv_weight],
        [block, block, ((1, *kv_shape[0]), bf16), block, own_rows, block]
        + [several(2, q_load), several(2, kv_load)],
        [
            pltpu.VMEM(*several(2, q_load)),
            pltpu.VMEM(*several(2, kv_load)),
            pltpu.VMEM(*run_shape),
            pltpu.VMEM(*half_tall),
            pltpu.VMEM(*p_shapes[0]),
            pltpu.SemaphoreType.DMA((4, 2)),
        ],
        20,
    )
    got = swap(send, 1)
    send2, keep2 = call(
        early_second, "early_second", [VMEM] * 5, [dq, own, do, wq, wkv], [block] * 2, [], 8
    )
    got2 = swap(send2, 1)
    step = BLOCK // PIECES
    cuts = [slice(i * step, (i + 1) * step) for i in range(PIECES)]
    pieces = [swap(total_of(keep[cut], got[cut]), 2) for cut in cuts]
    (early_dx,) = call(
        finish,
        "finish",
        [VMEM] * (2 + PIECES),
        [keep2, got2, *pieces],
        [((1, BLOCK, WIDTH), bf16)],
        [],
        8,
    )
    return (early_dx, carry)


def solution(mesh):
    in_specs = (
        P("section", None, None, "tp"),
        P("section", None, "tp"),
        P("section", None, "tp"),
        P("section", None, "tp"),
        P("section"),
        P("section", None, "tp"),
        P("section", None, "tp"),
        P(None, "tp"),
    )
    out_specs = (P("section", None, "tp"), P("section", None, "tp"))
    return jax.shard_map(local, mesh=mesh, in_specs=in_specs, out_specs=out_specs, check_vma=False)
```

```python
import functools
import math

import jax
import jax.numpy as jnp
from jax import lax
from jax.experimental import pallas as pl
from jax.experimental.pallas import tpu as pltpu
from jax.sharding import PartitionSpec as P

HD = 128
BLOCK = 256
WIDTH = 1024
KV_WIDTH = 256
HALVES = ((128, 256), (0, 128))
PIECES = 4
NT = (((1,), (1,)), ((), ()))
NN = (((1,), (0,)), ((), ()))


def dot(a, b, dims=NN):
    return lax.dot_general(a, b, dims, preferred_element_type=jnp.float32)


def tall(ref, rows_at, out):
    heads = ref.shape[-1] // HD
    rows = rows_at.stop - rows_at.start
    for h in range(heads):
        out[h * rows : (h + 1) * rows] = ref[rows_at, h * HD : (h + 1) * HD]


def probabilities(key_rows, q_g, bias):
    scale = math.log2(math.e) / math.sqrt(HD)
    s = dot(key_rows, q_g, NT) * scale + bias
    e = jnp.exp2(s - jnp.max(s, axis=0, keepdims=True))
    return e * (1.0 / jnp.sum(e, axis=0, keepdims=True))


def visible_bias(keys, first_row, rows, lanes):
    position = first_row + lax.rem(lax.broadcasted_iota(jnp.int32, (keys, lanes), 1), rows)
    key_at = lax.broadcasted_iota(jnp.int32, (keys, lanes), 0)
    return jnp.where(key_at <= position, 0.0, -1e30)


def grad_scores(p, dp):
    delta = jnp.sum(p * dp, axis=0, keepdims=True)
    return (p * (dp - delta)).astype(jnp.bfloat16)


def add_terms(keys, kv_ref, q_all, do_all, p_all, ds_all, running, dq_ref, dq_rows):
    rows = dq_rows.stop - dq_rows.start
    scale = 1.0 / math.sqrt(HD)
    ds = ds_all[:keys]
    running[:keys, :HD] += dot(ds, q_all[...]) * scale
    running[:keys, HD:] += dot(p_all[:keys], do_all[...])
    keys_t = kv_ref[:keys, :HD].astype(jnp.float32).T.astype(jnp.bfloat16)
    dq = dot(keys_t, ds) * scale
    for h in range(dq.shape[1] // rows):
        piece = dq[:, h * rows : (h + 1) * rows].T
        dq_ref[dq_rows, h * HD : (h + 1) * HD] = piece.astype(jnp.bfloat16)


def start_all(copies):
    for copy in copies:
        copy.start()


def wait_all(copies):
    for copy in copies:
        copy.wait()


def weight_loads(shards, wq_hbm, wkv_hbm, wq, wkv, sem):
    loads = []
    for i, shard in enumerate(shards):
        at = pl.ds(pl.multiple_of(shard * WIDTH, WIDTH), WIDTH)
        loads.append(pltpu.make_async_copy(wq_hbm.at[0, at], wq.at[i], sem.at[i, 0]))
        loads.append(pltpu.make_async_copy(wkv_hbm.at[0, at], wkv.at[i], sem.at[i, 1]))
    return loads


def project(dq, own, wq, wkv, slot):
    return dot(dq, wq[slot], NT) + dot(own, wkv[slot], NT)


def tall_loads(rows_of, lo, hi, out, sem):
    rows = hi - lo
    return [
        pltpu.make_async_copy(
            rows_of.at[lo:hi, h * HD : (h + 1) * HD], out.at[h * rows : (h + 1) * rows], sem.at[h]
        )
        for h in range(rows_of.shape[-1] // HD)
    ]


def wide(tall_ref, rows):
    heads = tall_ref.shape[0] // rows
    return jnp.concatenate([tall_ref[h * rows : (h + 1) * rows] for h in range(heads)], axis=1)


def late_first(
    block_ref, q_hbm, do_hbm, kv_hbm, carry_hbm, wq_hbm, wkv_hbm,
    send_ref, keep_ref, run_ref, dq_ref, own_ref, wq, wkv,
    kv_ref, carry, q_all, do_all, p_all, ds_all, sem, tall_sem, w_sem,
):
    tp = lax.axis_index("tp")
    kv_copy = pltpu.make_async_copy(kv_hbm.at[0], kv_ref, sem.at[0])
    carry_copy = pltpu.make_async_copy(carry_hbm.at[0], carry, sem.at[1])
    copies = tall_loads(q_hbm.at[0, 0], 0, BLOCK, q_all, tall_sem.at[0])
    copies += tall_loads(do_hbm.at[0], 0, BLOCK, do_all, tall_sem.at[1])
    loads = weight_loads((tp ^ 1, tp, tp ^ 3, tp ^ 2), wq_hbm, wkv_hbm, wq, wkv, w_sem)
    kv_copy.start()
    start_all(copies)
    carry_copy.start()
    first_row = (block_ref[0] + 1) * BLOCK
    keys = 3 * BLOCK
    bias = visible_bias(keys, first_row, BLOCK, BLOCK)
    kv_copy.wait()
    wait_all(copies)
    start_all(loads)
    for h in range(WIDTH // HD):
        at = slice(h * BLOCK, (h + 1) * BLOCK)
        p = probabilities(kv_ref[:, :HD], q_all[at], bias)
        p_all[:, at] = p.astype(jnp.bfloat16)
        ds_all[:, at] = grad_scores(p, dot(kv_ref[:, HD:], do_all[at], NT))
    carry_copy.wait()
    run_ref[...] = carry[...].astype(jnp.float32)
    add_terms(
        keys, kv_ref, q_all, do_all, p_all, ds_all, run_ref, dq_ref, slice(0, BLOCK)
    )
    own_ref[...] = run_ref[pl.ds(pl.multiple_of(first_row, BLOCK), BLOCK), :].astype(jnp.bfloat16)
    wait_all(loads)
    dq, own = dq_ref[...], own_ref[...]
    send_ref[...] = project(dq, own, wq, wkv, 0).astype(jnp.bfloat16)
    keep = project(dq, own, wq, wkv, 1) + wide(do_all, BLOCK).astype(jnp.float32)
    keep_ref[...] = keep.astype(jnp.bfloat16)


def late_second(dq_ref, own_ref, wq, wkv, send_ref, keep_ref):
    dq, own = dq_ref[...], own_ref[...]
    send_ref[...] = project(dq, own, wq, wkv, 2).astype(jnp.bfloat16)
    keep_ref[...] = project(dq, own, wq, wkv, 3).astype(jnp.bfloat16)


def early_probabilities(
    block_ref, q_hbm, kv_hbm, top_hbm, p_b, p_t, q_b, q_t, kv_ref, top_ref, sem, tall_sem
):
    copies = [pltpu.make_async_copy(kv_hbm.at[0], kv_ref, sem.at[0])]
    for n, ((lo, hi), q_all) in enumerate(zip(HALVES, (q_b, q_t))):
        copies += tall_loads(q_hbm.at[0, 1], lo, hi, q_all, tall_sem.at[n])
    top_copy = pltpu.make_async_copy(top_hbm, top_ref, sem.at[1])
    start_all(copies)
    top_copy.start()
    wait_all(copies)
    for (lo, hi), p_ref, q_all in zip(HALVES, (p_b, p_t), (q_b, q_t)):
        rows = hi - lo
        keys = BLOCK + hi
        bias = visible_bias(keys, block_ref[0] * BLOCK + lo, rows, 2 * rows)
        for base in range(0, q_all.shape[0], 2 * rows):
            at = slice(base, base + 2 * rows)
            p = probabilities(kv_ref[:keys, :HD], q_all[at], bias)
            p_ref[:, at] = p.astype(jnp.bfloat16)
    top_copy.wait()


def early_terms(half, passed, top_ref, kv_ref, q_all, p_ref, run_ref, do_ref, do_all, ds_all, dq_ref):
    lo, hi = half
    rows = hi - lo
    keys = BLOCK + hi
    is_last = lax.axis_index("section") == lax.axis_size("section") - 1
    do_ref[...] = jnp.where(is_last, top_ref[lo:hi], passed)
    tall(do_ref, slice(0, rows), do_all)
    for base in range(0, do_all.shape[0], 2 * rows):
        at = slice(base, base + 2 * rows)
        p = p_ref[:, at].astype(jnp.float32)
        ds_all[:keys, at] = grad_scores(p, dot(kv_ref[:keys, HD:], do_all[at], NT))
    add_terms(keys, kv_ref, q_all, do_all, p_ref, ds_all, run_ref, dq_ref, slice(0, rows))


def own_rows_of(running, first_row, rows):
    at = pl.ds(pl.multiple_of(first_row, BLOCK // 2), rows)
    return running[at, :].astype(jnp.bfloat16)


def project_all(dq, own, do_ref, wq, wkv, outs):
    for slot, out in zip((2, 3, 0, 1), outs):
        total = project(dq, own, wq, wkv, slot)
        if slot == 1:
            total = total + do_ref[...].astype(jnp.float32)
        out[...] = total.astype(jnp.bfloat16)


def early_bottom(
    block_ref, do_in, do_more, top_ref, kv_ref, q_all, p_ref, run_in, wq, wkv,
    send_ref, keep_ref, send2, keep2, run_ref,
    dq_ref, do_ref, do_all, ds_all,
):
    lo, hi = HALVES[0]
    passed = do_in[...].astype(jnp.float32) + do_more[...].astype(jnp.float32)
    run_ref[...] = run_in[...]
    early_terms(HALVES[0], passed.astype(jnp.bfloat16), top_ref, kv_ref, q_all, p_ref, run_ref,
                do_ref, do_all, ds_all, dq_ref)
    own = own_rows_of(run_ref, block_ref[0] * BLOCK + lo, hi - lo)
    project_all(dq_ref[...], own, do_ref, wq, wkv, (send_ref, keep_ref, send2, keep2))


def early_top(
    block_ref, do_in, top_ref, kv_ref, q_all, p_ref, run_in, wq, wkv,
    send_ref, keep_ref, send2, keep2, carry_ref,
    dq_ref, do_ref, running, do_all, ds_all,
):
    lo, hi = HALVES[1]
    running[...] = run_in[...]
    early_terms(HALVES[1], do_in[...], top_ref, kv_ref, q_all, p_ref, running,
                do_ref, do_all, ds_all, dq_ref)
    first_row = block_ref[0] * BLOCK
    own = own_rows_of(running, first_row + lo, hi - lo)
    project_all(dq_ref[...], own, do_ref, wq, wkv, (send_ref, keep_ref, send2, keep2))
    below = lax.broadcasted_iota(jnp.int32, running.shape, 0) < first_row
    carry_ref[0] = jnp.where(below, running[...], 0.0).astype(jnp.bfloat16)


def finish(keep_t, got_t, keep_b, got_b, *refs):
    *pieces, out_ref = refs
    rows = pieces[0].shape[0]
    half = len(pieces) // 2
    for i, piece in enumerate(pieces):
        keep, got = (keep_t, got_t) if i < half else (keep_b, got_b)
        at = slice(i % half * rows, (i % half + 1) * rows)
        out_ref[0, i * rows : (i + 1) * rows] = total_of(keep[at], got[at], piece[...])


def add_rows(*refs):
    *ins, out_ref = refs
    out_ref[...] = total_of(*(ref[...] for ref in ins))


def add_halves(a_ref, b_ref, top_ref, bottom_ref):
    half = top_ref.shape[0]
    top_ref[...] = total_of(a_ref[:half], b_ref[:half])
    bottom_ref[...] = total_of(a_ref[half:], b_ref[half:])


SMEM = pl.BlockSpec(memory_space=pltpu.SMEM)
HBM = pl.BlockSpec(memory_space=pltpu.HBM)
VMEM = pl.BlockSpec(memory_space=pltpu.VMEM)


def call(kernel, name, specs, args, outs, scratch, megabytes):
    args = [
        pltpu.with_memory_space_constraint(arg, pltpu.HBM) if spec is HBM else arg
        for arg, spec in zip(args, specs)
    ]
    return pl.pallas_call(
        kernel,
        out_shape=[
            pltpu.HBM(*out[:2]) if len(out) > 2 else jax.ShapeDtypeStruct(*out) for out in outs
        ],
        in_specs=specs,
        out_specs=[HBM if len(out) > 2 else VMEM for out in outs],
        scratch_shapes=scratch,
        compiler_params=pltpu.CompilerParams(vmem_limit_bytes=megabytes * 1024 * 1024),
        cost_estimate=pl.CostEstimate(
            flops=2 * 10**9, bytes_accessed=10**6, transcendentals=0
        ),
        name=name,
    )(*args)


def add(name, *terms):
    shape = terms[0].shape
    (out,) = call(
        add_rows, name, [VMEM] * len(terms), terms, [(shape, jnp.bfloat16)], [], 4
    )
    return out


def swap(block, mask):
    return lax.ppermute(block, "tp", [(i, i ^ mask) for i in range(lax.axis_size("tp"))])


def shift_down(block, mask):
    sections, tp = lax.axis_size("section"), lax.axis_size("tp")
    route = [
        (s * tp + t, (s - 1) % sections * tp + (t ^ mask))
        for s in range(sections)
        for t in range(tp)
    ]
    return lax.ppermute(block, ("section", "tp"), route)


def total_of(*terms):
    out = terms[0].astype(jnp.float32)
    for term in terms[1:]:
        out = out + term.astype(jnp.float32)
    return out.astype(jnp.bfloat16)


def local(query, keyval, q_weight, kv_weight, block_index, carry_in, grad_late, grad_top):
    length = keyval.shape[1]
    half = BLOCK // 2
    tall_rows = BLOCK * WIDTH // HD
    bf16, f32 = jnp.bfloat16, jnp.float32
    block = ((BLOCK, WIDTH), bf16)
    half_block = ((half, WIDTH), bf16)
    half_tall = ((tall_rows // 2, HD), bf16)
    own_rows = ((BLOCK, KV_WIDTH), bf16)
    run_shape = ((length, KV_WIDTH), f32)
    kv_shape = ((length, KV_WIDTH), bf16)
    p_shapes = [((BLOCK + hi, tall_rows // 2), bf16) for _, hi in HALVES]
    q_load, kv_load = ((WIDTH, WIDTH), bf16), ((WIDTH, KV_WIDTH), bf16)
    several = lambda n, shape: ((n, *shape[0]), shape[1])
    send, keep, run, dq, own, wq, wkv = call(
        late_first,
        "late_first",
        [SMEM] + [HBM] * 6,
        [block_index, query, grad_late, keyval, carry_in, q_weight, kv_weight],
        [block, block, run_shape, block, own_rows]
        + [several(4, q_load), several(4, kv_load)],
        [
            pltpu.VMEM(*kv_shape),
            pltpu.VMEM(*kv_shape),
            pltpu.VMEM((tall_rows, HD), bf16),
            pltpu.VMEM((tall_rows, HD), bf16),
            pltpu.VMEM((length, tall_rows), bf16),
            pltpu.VMEM((length, tall_rows), bf16),
            pltpu.SemaphoreType.DMA((2,)),
            pltpu.SemaphoreType.DMA((2, WIDTH // HD)),
            pltpu.SemaphoreType.DMA((4, 2)),
        ],
        20,
    )
    got = swap(send, 1)
    send2, keep2 = call(
        late_second, "late_second", [VMEM] * 4, [dq, own, wq, wkv], [block] * 2, [], 8
    )
    got2 = swap(send2, 1)
    mine_t, mine_b = call(
        add_halves, "add_mine", [VMEM] * 2, [keep, got], [half_block] * 2, [], 4
    )
    straight = shift_down(mine_b, 0)
    other = swap(mine_t, 2)
    kept, crossed = call(
        add_halves, "add_crossed", [VMEM] * 2, [keep2, got2], [half_block, half_block], [], 4
    )
    crossed = shift_down(crossed, 2)
    summed = shift_down(add("add_summed", kept, other), 2)
    p_b, p_t, q_b, q_t, kv_held, top_held = call(
        early_probabilities,
        "early_probabilities",
        [SMEM, HBM, HBM, HBM],
        [block_index, query, keyval, grad_top],
        [*p_shapes, half_tall, half_tall, kv_shape, block],
        [pltpu.SemaphoreType.DMA((2,)), pltpu.SemaphoreType.DMA((2, WIDTH // HD))],
        10,
    )
    half_scratch = [
        pltpu.VMEM(*half_block),
        pltpu.VMEM(*half_block),
        pltpu.VMEM(*half_tall),
        pltpu.VMEM(*p_shapes[0]),
    ]
    send_b, keep_b, send2_b, keep2_b, run = call(
        early_bottom,
        "early_bottom",
        [SMEM] + [VMEM] * 9,
        [block_index, straight, crossed, top_held, kv_held, q_b, p_b, run, wq, wkv],
        [half_block] * 4 + [run_shape],
        half_scratch,
        10,
    )
    got_b, got2_b = swap(send_b, 1), swap(send2_b, 1)
    send_t, keep_t, send2_t, keep2_t, carry = call(
        early_top,
        "early_top",
        [SMEM] + [VMEM] * 8,
        [block_index, summed, top_held, kv_held, q_t, p_t, run, wq, wkv],
        [half_block] * 4 + [((1, *kv_shape[0]), bf16)],
        half_scratch[:2] + [pltpu.VMEM(*run_shape)] + half_scratch[2:],
        10,
    )
    got_t, got2_t = swap(send_t, 1), swap(send2_t, 1)
    step = BLOCK // PIECES
    cuts = [slice(i * step, (i + 1) * step) for i in range(half // step)]
    from_b = [swap(total_of(keep_b[cut], got_b[cut]), 2) for cut in cuts]
    from_t = [swap(total_of(keep_t[cut], got_t[cut]), 2) for cut in cuts]
    (early_dx,) = call(
        finish,
        "finish",
        [VMEM] * (4 + PIECES),
        [keep2_t, got2_t, keep2_b, got2_b, *from_t, *from_b],
        [((1, BLOCK, WIDTH), bf16)],
        [],
        8,
    )
    return (early_dx, carry)


def solution(mesh):
    in_specs = (
        P("section", None, None, "tp"),
        P("section", None, "tp"),
        P("section", None, "tp"),
        P("section", None, "tp"),
        P("section"),
        P("section", None, "tp"),
        P("section", None, "tp"),
        P(None, "tp"),
    )
    out_specs = (P("section", None, "tp"), P("section", None, "tp"))
    return jax.shard_map(local, mesh=mesh, in_specs=in_specs, out_specs=out_specs, check_vma=False)
```

```python
import functools
import math

import jax
import jax.numpy as jnp
from jax import lax
from jax.experimental import pallas as pl
from jax.experimental.pallas import tpu as pltpu
from jax.sharding import PartitionSpec as P

HD = 128
BLOCK = 256
WIDTH = 1024
KV_WIDTH = 256
HALVES = ((128, 256), (0, 128))
PIECES = 2
NT = (((1,), (1,)), ((), ()))
NN = (((1,), (0,)), ((), ()))


def dot(a, b, dims=NN):
    return lax.dot_general(a, b, dims, preferred_element_type=jnp.float32)


def tall(ref, rows_at, out):
    heads = ref.shape[-1] // HD
    rows = rows_at.stop - rows_at.start
    for h in range(heads):
        out[h * rows : (h + 1) * rows] = ref[rows_at, h * HD : (h + 1) * HD]


def probabilities(key_rows, q_g, bias):
    scale = math.log2(math.e) / math.sqrt(HD)
    s = dot(key_rows, q_g, NT) * scale + bias
    e = jnp.exp2(s - jnp.max(s, axis=0, keepdims=True))
    return e * (1.0 / jnp.sum(e, axis=0, keepdims=True))


def visible_bias(keys, first_row, rows, lanes):
    position = first_row + lax.rem(lax.broadcasted_iota(jnp.int32, (keys, lanes), 1), rows)
    key_at = lax.broadcasted_iota(jnp.int32, (keys, lanes), 0)
    return jnp.where(key_at <= position, 0.0, -1e30)


def grad_scores(p, dp):
    delta = jnp.sum(p * dp, axis=0, keepdims=True)
    return (p * (dp - delta)).astype(jnp.bfloat16)


def add_terms(keys, kv_ref, q_all, do_all, p_all, ds_all, running, dq_ref, dq_rows):
    rows = dq_rows.stop - dq_rows.start
    scale = 1.0 / math.sqrt(HD)
    ds = ds_all[:keys]
    running[:keys, :HD] += dot(ds, q_all[...]) * scale
    running[:keys, HD:] += dot(p_all[:keys], do_all[...])
    keys_t = kv_ref[:keys, :HD].astype(jnp.float32).T.astype(jnp.bfloat16)
    dq = dot(keys_t, ds) * scale
    for h in range(dq.shape[1] // rows):
        piece = dq[:, h * rows : (h + 1) * rows].T
        dq_ref[dq_rows, h * HD : (h + 1) * HD] = piece.astype(jnp.bfloat16)


def start_all(copies):
    for copy in copies:
        copy.start()


def wait_all(copies):
    for copy in copies:
        copy.wait()


def weight_loads(shards, wq_hbm, wkv_hbm, wq, wkv, sem):
    loads = []
    for i, shard in enumerate(shards):
        at = pl.ds(pl.multiple_of(shard * WIDTH, WIDTH), WIDTH)
        loads.append(pltpu.make_async_copy(wq_hbm.at[0, at], wq.at[i], sem.at[i, 0]))
        loads.append(pltpu.make_async_copy(wkv_hbm.at[0, at], wkv.at[i], sem.at[i, 1]))
    return loads


def project(dq, own, wq, wkv, slot):
    return dot(dq, wq[slot], NT) + dot(own, wkv[slot], NT)


def tall_loads(rows_of, lo, hi, out, sem):
    rows = hi - lo
    return [
        pltpu.make_async_copy(
            rows_of.at[lo:hi, h * HD : (h + 1) * HD], out.at[h * rows : (h + 1) * rows], sem.at[h]
        )
        for h in range(rows_of.shape[-1] // HD)
    ]


def wide(tall_ref, rows):
    heads = tall_ref.shape[0] // rows
    return jnp.concatenate([tall_ref[h * rows : (h + 1) * rows] for h in range(heads)], axis=1)


def late_first(
    block_ref, q_hbm, do_hbm, kv_hbm, carry_hbm, wq_hbm, wkv_hbm,
    send_ref, keep_ref, run_ref, dq_ref, own_ref, wq, wkv,
    kv_ref, carry, q_all, do_all, p_all, ds_all, sem, tall_sem, w_sem,
):
    tp = lax.axis_index("tp")
    kv_copy = pltpu.make_async_copy(kv_hbm.at[0], kv_ref, sem.at[0])
    carry_copy = pltpu.make_async_copy(carry_hbm.at[0], carry, sem.at[1])
    copies = tall_loads(q_hbm.at[0, 0], 0, BLOCK, q_all, tall_sem.at[0])
    copies += tall_loads(do_hbm.at[0], 0, BLOCK, do_all, tall_sem.at[1])
    loads = weight_loads((tp ^ 1, tp, tp ^ 3, tp ^ 2), wq_hbm, wkv_hbm, wq, wkv, w_sem)
    kv_copy.start()
    start_all(copies)
    carry_copy.start()
    first_row = (block_ref[0] + 1) * BLOCK
    keys = 3 * BLOCK
    bias = visible_bias(keys, first_row, BLOCK, BLOCK)
    kv_copy.wait()
    wait_all(copies)
    start_all(loads)
    for h in range(WIDTH // HD):
        at = slice(h * BLOCK, (h + 1) * BLOCK)
        p = probabilities(kv_ref[:, :HD], q_all[at], bias)
        p_all[:, at] = p.astype(jnp.bfloat16)
        ds_all[:, at] = grad_scores(p, dot(kv_ref[:, HD:], do_all[at], NT))
    carry_copy.wait()
    run_ref[...] = carry[...].astype(jnp.float32)
    add_terms(
        keys, kv_ref, q_all, do_all, p_all, ds_all, run_ref, dq_ref, slice(0, BLOCK)
    )
    own_ref[...] = run_ref[pl.ds(pl.multiple_of(first_row, BLOCK), BLOCK), :].astype(jnp.bfloat16)
    wait_all(loads)
    dq, own = dq_ref[...], own_ref[...]
    send_ref[...] = project(dq, own, wq, wkv, 0).astype(jnp.bfloat16)
    keep = project(dq, own, wq, wkv, 1) + wide(do_all, BLOCK).astype(jnp.float32)
    keep_ref[...] = keep.astype(jnp.bfloat16)


def late_second(dq_ref, own_ref, wq, wkv, send_ref, keep_ref):
    dq, own = dq_ref[...], own_ref[...]
    send_ref[...] = project(dq, own, wq, wkv, 2).astype(jnp.bfloat16)
    keep_ref[...] = project(dq, own, wq, wkv, 3).astype(jnp.bfloat16)


def early_probabilities(
    block_ref, q_hbm, kv_hbm, top_hbm, p_b, p_t, q_b, q_t, kv_ref, top_ref, sem, tall_sem
):
    copies = [pltpu.make_async_copy(kv_hbm.at[0], kv_ref, sem.at[0])]
    for n, ((lo, hi), q_all) in enumerate(zip(HALVES, (q_b, q_t))):
        copies += tall_loads(q_hbm.at[0, 1], lo, hi, q_all, tall_sem.at[n])
    top_copy = pltpu.make_async_copy(top_hbm, top_ref, sem.at[1])
    start_all(copies)
    top_copy.start()
    wait_all(copies)
    for (lo, hi), p_ref, q_all in zip(HALVES, (p_b, p_t), (q_b, q_t)):
        rows = hi - lo
        keys = BLOCK + hi
        bias = visible_bias(keys, block_ref[0] * BLOCK + lo, rows, 2 * rows)
        for base in range(0, q_all.shape[0], 2 * rows):
            at = slice(base, base + 2 * rows)
            p = probabilities(kv_ref[:keys, :HD], q_all[at], bias)
            p_ref[:, at] = p.astype(jnp.bfloat16)
    top_copy.wait()


def early_terms(half, passed, top_ref, kv_ref, q_all, p_ref, run_ref, do_ref, do_all, ds_all, dq_ref):
    lo, hi = half
    rows = hi - lo
    keys = BLOCK + hi
    is_last = lax.axis_index("section") == lax.axis_size("section") - 1
    do_ref[...] = jnp.where(is_last, top_ref[lo:hi], passed)
    tall(do_ref, slice(0, rows), do_all)
    for base in range(0, do_all.shape[0], 2 * rows):
        at = slice(base, base + 2 * rows)
        p = p_ref[:, at].astype(jnp.float32)
        ds_all[:keys, at] = grad_scores(p, dot(kv_ref[:keys, HD:], do_all[at], NT))
    add_terms(keys, kv_ref, q_all, do_all, p_ref, ds_all, run_ref, dq_ref, slice(0, rows))


def own_rows_of(running, first_row, rows):
    at = pl.ds(pl.multiple_of(first_row, BLOCK // 2), rows)
    return running[at, :].astype(jnp.bfloat16)


def project_all(dq, own, do_ref, wq, wkv, outs):
    for slot, out in zip((2, 3, 0, 1), outs):
        total = project(dq, own, wq, wkv, slot)
        if slot == 1:
            total = total + do_ref[...].astype(jnp.float32)
        out[...] = total.astype(jnp.bfloat16)


def early_bottom(
    block_ref, do_in, do_more, top_ref, kv_ref, q_all, p_ref, run_in, wq, wkv,
    send_ref, keep_ref, send2, keep2, run_ref,
    dq_ref, do_ref, do_all, ds_all,
):
    lo, hi = HALVES[0]
    passed = do_in[...].astype(jnp.float32) + do_more[...].astype(jnp.float32)
    run_ref[...] = run_in[...]
    early_terms(HALVES[0], passed.astype(jnp.bfloat16), top_ref, kv_ref, q_all, p_ref, run_ref,
                do_ref, do_all, ds_all, dq_ref)
    own = own_rows_of(run_ref, block_ref[0] * BLOCK + lo, hi - lo)
    project_all(dq_ref[...], own, do_ref, wq, wkv, (send_ref, keep_ref, send2, keep2))


def early_top(
    block_ref, do_in, top_ref, kv_ref, q_all, p_ref, run_in, wq, wkv,
    send_ref, keep_ref, send2, keep2, carry_ref,
    dq_ref, do_ref, running, do_all, ds_all,
):
    lo, hi = HALVES[1]
    running[...] = run_in[...]
    early_terms(HALVES[1], do_in[...], top_ref, kv_ref, q_all, p_ref, running,
                do_ref, do_all, ds_all, dq_ref)
    first_row = block_ref[0] * BLOCK
    own = own_rows_of(running, first_row + lo, hi - lo)
    project_all(dq_ref[...], own, do_ref, wq, wkv, (send_ref, keep_ref, send2, keep2))
    below = lax.broadcasted_iota(jnp.int32, running.shape, 0) < first_row
    carry_ref[0] = jnp.where(below, running[...], 0.0).astype(jnp.bfloat16)


def finish(keep_t, got_t, keep_b, got_b, *refs):
    *pieces, out_ref = refs
    rows = pieces[0].shape[0]
    half = len(pieces) // 2
    for i, piece in enumerate(pieces):
        keep, got = (keep_t, got_t) if i < half else (keep_b, got_b)
        at = slice(i % half * rows, (i % half + 1) * rows)
        out_ref[0, i * rows : (i + 1) * rows] = total_of(keep[at], got[at], piece[...])


def add_rows(*refs):
    *ins, out_ref = refs
    out_ref[...] = total_of(*(ref[...] for ref in ins))


def add_halves(a_ref, b_ref, top_ref, bottom_ref):
    half = top_ref.shape[0]
    top_ref[...] = total_of(a_ref[:half], b_ref[:half])
    bottom_ref[...] = total_of(a_ref[half:], b_ref[half:])


SMEM = pl.BlockSpec(memory_space=pltpu.SMEM)
HBM = pl.BlockSpec(memory_space=pltpu.HBM)
VMEM = pl.BlockSpec(memory_space=pltpu.VMEM)


def call(kernel, name, specs, args, outs, scratch, megabytes):
    args = [
        pltpu.with_memory_space_constraint(arg, pltpu.HBM) if spec is HBM else arg
        for arg, spec in zip(args, specs)
    ]
    return pl.pallas_call(
        kernel,
        out_shape=[
            pltpu.HBM(*out[:2]) if len(out) > 2 else jax.ShapeDtypeStruct(*out) for out in outs
        ],
        in_specs=specs,
        out_specs=[HBM if len(out) > 2 else VMEM for out in outs],
        scratch_shapes=scratch,
        compiler_params=pltpu.CompilerParams(vmem_limit_bytes=megabytes * 1024 * 1024),
        cost_estimate=pl.CostEstimate(
            flops=2 * 10**9, bytes_accessed=10**6, transcendentals=0
        ),
        name=name,
    )(*args)


def add(name, *terms):
    shape = terms[0].shape
    (out,) = call(
        add_rows, name, [VMEM] * len(terms), terms, [(shape, jnp.bfloat16)], [], 4
    )
    return out


def swap(block, mask):
    return lax.ppermute(block, "tp", [(i, i ^ mask) for i in range(lax.axis_size("tp"))])


def shift_down(block, mask):
    sections, tp = lax.axis_size("section"), lax.axis_size("tp")
    route = [
        (s * tp + t, (s - 1) % sections * tp + (t ^ mask))
        for s in range(sections)
        for t in range(tp)
    ]
    return lax.ppermute(block, ("section", "tp"), route)


def total_of(*terms):
    out = terms[0].astype(jnp.float32)
    for term in terms[1:]:
        out = out + term.astype(jnp.float32)
    return out.astype(jnp.bfloat16)


def local(query, keyval, q_weight, kv_weight, block_index, carry_in, grad_late, grad_top):
    length = keyval.shape[1]
    half = BLOCK // 2
    tall_rows = BLOCK * WIDTH // HD
    bf16, f32 = jnp.bfloat16, jnp.float32
    block = ((BLOCK, WIDTH), bf16)
    half_block = ((half, WIDTH), bf16)
    half_tall = ((tall_rows // 2, HD), bf16)
    own_rows = ((BLOCK, KV_WIDTH), bf16)
    run_shape = ((length, KV_WIDTH), f32)
    kv_shape = ((length, KV_WIDTH), bf16)
    p_shapes = [((BLOCK + hi, tall_rows // 2), bf16) for _, hi in HALVES]
    q_load, kv_load = ((WIDTH, WIDTH), bf16), ((WIDTH, KV_WIDTH), bf16)
    several = lambda n, shape: ((n, *shape[0]), shape[1])
    send, keep, run, dq, own, wq, wkv = call(
        late_first,
        "late_first",
        [SMEM] + [HBM] * 6,
        [block_index, query, grad_late, keyval, carry_in, q_weight, kv_weight],
        [block, block, run_shape, block, own_rows]
        + [several(4, q_load), several(4, kv_load)],
        [
            pltpu.VMEM(*kv_shape),
            pltpu.VMEM(*kv_shape),
            pltpu.VMEM((tall_rows, HD), bf16),
            pltpu.VMEM((tall_rows, HD), bf16),
            pltpu.VMEM((length, tall_rows), bf16),
            pltpu.VMEM((length, tall_rows), bf16),
            pltpu.SemaphoreType.DMA((2,)),
            pltpu.SemaphoreType.DMA((2, WIDTH // HD)),
            pltpu.SemaphoreType.DMA((4, 2)),
        ],
        20,
    )
    got = swap(send, 1)
    send2, keep2 = call(
        late_second, "late_second", [VMEM] * 4, [dq, own, wq, wkv], [block] * 2, [], 8
    )
    got2 = swap(send2, 1)
    mine_t, mine_b = call(
        add_halves, "add_mine", [VMEM] * 2, [keep, got], [half_block] * 2, [], 4
    )
    straight = shift_down(mine_b, 0)
    other = swap(mine_t, 2)
    kept, crossed = call(
        add_halves, "add_crossed", [VMEM] * 2, [keep2, got2], [half_block, half_block], [], 4
    )
    crossed = shift_down(crossed, 2)
    p_b, p_t, q_b, q_t, kv_held, top_held = call(
        early_probabilities,
        "early_probabilities",
        [SMEM, HBM, HBM, HBM],
        [block_index, query, keyval, grad_top],
        [*p_shapes, half_tall, half_tall, kv_shape, block],
        [pltpu.SemaphoreType.DMA((2,)), pltpu.SemaphoreType.DMA((2, WIDTH // HD))],
        10,
    )
    kept, p_t = lax.optimization_barrier((kept, p_t))
    summed = shift_down(add("add_summed", kept, other), 2)
    half_scratch = [
        pltpu.VMEM(*half_block),
        pltpu.VMEM(*half_block),
        pltpu.VMEM(*half_tall),
        pltpu.VMEM(*p_shapes[0]),
    ]
    send_b, keep_b, send2_b, keep2_b, run = call(
        early_bottom,
        "early_bottom",
        [SMEM] + [VMEM] * 9,
        [block_index, straight, crossed, top_held, kv_held, q_b, p_b, run, wq, wkv],
        [half_block] * 4 + [run_shape],
        half_scratch,
        10,
    )
    got_b, got2_b = swap(send_b, 1), swap(send2_b, 1)
    send_t, keep_t, send2_t, keep2_t, carry = call(
        early_top,
        "early_top",
        [SMEM] + [VMEM] * 8,
        [block_index, summed, top_held, kv_held, q_t, p_t, run, wq, wkv],
        [half_block] * 4 + [((1, *kv_shape[0]), bf16)],
        half_scratch[:2] + [pltpu.VMEM(*run_shape)] + half_scratch[2:],
        10,
    )
    got_t, got2_t = swap(send_t, 1), swap(send2_t, 1)
    step = BLOCK // PIECES
    cuts = [slice(i * step, (i + 1) * step) for i in range(half // step)]
    from_b = [swap(total_of(keep_b[cut], got_b[cut]), 2) for cut in cuts]
    from_t = [swap(total_of(keep_t[cut], got_t[cut]), 2) for cut in cuts]
    (early_dx,) = call(
        finish,
        "finish",
        [VMEM] * (4 + PIECES),
        [keep2_t, got2_t, keep2_b, got2_b, *from_t, *from_b],
        [((1, BLOCK, WIDTH), bf16)],
        [],
        8,
    )
    return (early_dx, carry)


def solution(mesh):
    in_specs = (
        P("section", None, None, "tp"),
        P("section", None, "tp"),
        P("section", None, "tp"),
        P("section", None, "tp"),
        P("section"),
        P("section", None, "tp"),
        P("section", None, "tp"),
        P(None, "tp"),
    )
    out_specs = (P("section", None, "tp"), P("section", None, "tp"))
    return jax.shard_map(local, mesh=mesh, in_specs=in_specs, out_specs=out_specs, check_vma=False)
```

```python
import functools
import math

import jax
import jax.numpy as jnp
from jax import lax
from jax.experimental import pallas as pl
from jax.experimental.pallas import tpu as pltpu
from jax.sharding import PartitionSpec as P

HD = 128
BLOCK = 256
WIDTH = 1024
KV_WIDTH = 256
HALVES = ((128, 256), (0, 128))
PIECES = 2
NT = (((1,), (1,)), ((), ()))
NN = (((1,), (0,)), ((), ()))


def dot(a, b, dims=NN):
    return lax.dot_general(a, b, dims, preferred_element_type=jnp.float32)


def tall(ref, rows_at, out):
    heads = ref.shape[-1] // HD
    rows = rows_at.stop - rows_at.start
    for h in range(heads):
        out[h * rows : (h + 1) * rows] = ref[rows_at, h * HD : (h + 1) * HD]


def probabilities(key_rows, q_g, bias):
    scale = math.log2(math.e) / math.sqrt(HD)
    s = dot(key_rows, q_g, NT) * scale
    always = s.shape[0] - bias.shape[0]
    s = s + bias if always == 0 else jnp.concatenate([s[:always], s[always:] + bias], axis=0)
    e = jnp.exp2(s - jnp.max(s, axis=0, keepdims=True))
    return e * (1.0 / jnp.sum(e, axis=0, keepdims=True))


def visible_bias(keys, first_row, rows, lanes):
    position = first_row + lax.rem(lax.broadcasted_iota(jnp.int32, (keys, lanes), 1), rows)
    key_at = lax.broadcasted_iota(jnp.int32, (keys, lanes), 0)
    return jnp.where(key_at <= position, 0.0, -1e30)


def grad_scores(p, dp):
    delta = jnp.sum(p * dp, axis=0, keepdims=True)
    return (p * (dp - delta)).astype(jnp.bfloat16)


def add_terms(keys, kv_ref, q_all, do_all, p_all, ds_all, running, dq_ref, dq_rows):
    rows = dq_rows.stop - dq_rows.start
    scale = 1.0 / math.sqrt(HD)
    ds = ds_all[:keys]
    running[:keys, :HD] += dot(ds, q_all[...]) * scale
    running[:keys, HD:] += dot(p_all[:keys], do_all[...])
    keys_t = kv_ref[:keys, :HD].astype(jnp.float32).T.astype(jnp.bfloat16)
    dq = dot(keys_t, ds) * scale
    for h in range(dq.shape[1] // rows):
        piece = dq[:, h * rows : (h + 1) * rows].T
        dq_ref[dq_rows, h * HD : (h + 1) * HD] = piece.astype(jnp.bfloat16)


def start_all(copies):
    for copy in copies:
        copy.start()


def wait_all(copies):
    for copy in copies:
        copy.wait()


def weight_loads(shards, wq_hbm, wkv_hbm, wq, wkv, sem):
    loads = []
    for i, shard in enumerate(shards):
        at = pl.ds(pl.multiple_of(shard * WIDTH, WIDTH), WIDTH)
        loads.append(pltpu.make_async_copy(wq_hbm.at[0, at], wq.at[i], sem.at[i, 0]))
        loads.append(pltpu.make_async_copy(wkv_hbm.at[0, at], wkv.at[i], sem.at[i, 1]))
    return loads


def project(dq, own, wq, wkv, slot):
    return dot(dq, wq[slot], NT) + dot(own, wkv[slot], NT)


def tall_loads(rows_of, lo, hi, out, sem):
    rows = hi - lo
    return [
        pltpu.make_async_copy(
            rows_of.at[lo:hi, h * HD : (h + 1) * HD], out.at[h * rows : (h + 1) * rows], sem.at[h]
        )
        for h in range(rows_of.shape[-1] // HD)
    ]


def wide(tall_ref, rows):
    heads = tall_ref.shape[0] // rows
    return jnp.concatenate([tall_ref[h * rows : (h + 1) * rows] for h in range(heads)], axis=1)


def late_first(
    block_ref, q_hbm, do_hbm, kv_hbm, carry_hbm, wq_hbm, wkv_hbm,
    send_ref, keep_ref, run_ref, dq_ref, own_ref, wq, wkv,
    kv_ref, carry, q_all, do_all, p_all, ds_all, sem, tall_sem, w_sem,
):
    tp = lax.axis_index("tp")
    kv_copy = pltpu.make_async_copy(kv_hbm.at[0], kv_ref, sem.at[0])
    carry_copy = pltpu.make_async_copy(carry_hbm.at[0], carry, sem.at[1])
    copies = tall_loads(q_hbm.at[0, 0], 0, BLOCK, q_all, tall_sem.at[0])
    copies += tall_loads(do_hbm.at[0], 0, BLOCK, do_all, tall_sem.at[1])
    loads = weight_loads((tp ^ 1, tp, tp ^ 3, tp ^ 2), wq_hbm, wkv_hbm, wq, wkv, w_sem)
    kv_copy.start()
    start_all(copies)
    carry_copy.start()
    first_row = (block_ref[0] + 1) * BLOCK
    keys = 3 * BLOCK
    bias = visible_bias(keys - BLOCK, first_row - BLOCK, BLOCK, BLOCK)
    kv_copy.wait()
    wait_all(copies)
    start_all(loads)
    for h in range(WIDTH // HD):
        at = slice(h * BLOCK, (h + 1) * BLOCK)
        p = probabilities(kv_ref[:, :HD], q_all[at], bias)
        p_all[:, at] = p.astype(jnp.bfloat16)
        ds_all[:, at] = grad_scores(p, dot(kv_ref[:, HD:], do_all[at], NT))
    carry_copy.wait()
    run_ref[...] = carry[...].astype(jnp.float32)
    add_terms(
        keys, kv_ref, q_all, do_all, p_all, ds_all, run_ref, dq_ref, slice(0, BLOCK)
    )
    own_ref[...] = run_ref[pl.ds(pl.multiple_of(first_row, BLOCK), BLOCK), :].astype(jnp.bfloat16)
    wait_all(loads)
    dq, own = dq_ref[...], own_ref[...]
    send_ref[...] = project(dq, own, wq, wkv, 0).astype(jnp.bfloat16)
    keep = project(dq, own, wq, wkv, 1) + wide(do_all, BLOCK).astype(jnp.float32)
    keep_ref[...] = keep.astype(jnp.bfloat16)


def late_second(dq_ref, own_ref, wq, wkv, send_ref, keep_ref):
    dq, own = dq_ref[...], own_ref[...]
    send_ref[...] = project(dq, own, wq, wkv, 2).astype(jnp.bfloat16)
    keep_ref[...] = project(dq, own, wq, wkv, 3).astype(jnp.bfloat16)


def early_probabilities(
    block_ref, q_hbm, kv_hbm, top_hbm, p_b, p_t, q_b, q_t, kv_ref, top_ref, sem, tall_sem
):
    copies = [pltpu.make_async_copy(kv_hbm.at[0], kv_ref, sem.at[0])]
    for n, ((lo, hi), q_all) in enumerate(zip(HALVES, (q_b, q_t))):
        copies += tall_loads(q_hbm.at[0, 1], lo, hi, q_all, tall_sem.at[n])
    top_copy = pltpu.make_async_copy(top_hbm, top_ref, sem.at[1])
    start_all(copies)
    top_copy.start()
    wait_all(copies)
    for (lo, hi), p_ref, q_all in zip(HALVES, (p_b, p_t), (q_b, q_t)):
        rows = hi - lo
        keys = BLOCK + hi
        bias = visible_bias(keys, block_ref[0] * BLOCK + lo, rows, 2 * rows)
        for base in range(0, q_all.shape[0], 2 * rows):
            at = slice(base, base + 2 * rows)
            p = probabilities(kv_ref[:keys, :HD], q_all[at], bias)
            p_ref[:, at] = p.astype(jnp.bfloat16)
    top_copy.wait()


def early_terms(half, passed, top_ref, kv_ref, q_all, p_ref, run_ref, do_ref, do_all, ds_all, dq_ref):
    lo, hi = half
    rows = hi - lo
    keys = BLOCK + hi
    is_last = lax.axis_index("section") == lax.axis_size("section") - 1
    do_ref[...] = jnp.where(is_last, top_ref[lo:hi], passed)
    tall(do_ref, slice(0, rows), do_all)
    for base in range(0, do_all.shape[0], 2 * rows):
        at = slice(base, base + 2 * rows)
        p = p_ref[:, at].astype(jnp.float32)
        ds_all[:keys, at] = grad_scores(p, dot(kv_ref[:keys, HD:], do_all[at], NT))
    add_terms(keys, kv_ref, q_all, do_all, p_ref, ds_all, run_ref, dq_ref, slice(0, rows))


def own_rows_of(running, first_row, rows):
    at = pl.ds(pl.multiple_of(first_row, BLOCK // 2), rows)
    return running[at, :].astype(jnp.bfloat16)


def project_all(dq, own, do_ref, wq, wkv, outs):
    for slot, out in zip((2, 3, 0, 1), outs):
        total = project(dq, own, wq, wkv, slot)
        if slot == 1:
            total = total + do_ref[...].astype(jnp.float32)
        out[...] = total.astype(jnp.bfloat16)


def early_bottom(
    block_ref, do_in, do_more, top_ref, kv_ref, q_all, p_ref, run_in, wq, wkv,
    send_ref, keep_ref, send2, keep2, run_ref,
    dq_ref, do_ref, do_all, ds_all,
):
    lo, hi = HALVES[0]
    passed = do_in[...].astype(jnp.float32) + do_more[...].astype(jnp.float32)
    run_ref[...] = run_in[...]
    early_terms(HALVES[0], passed.astype(jnp.bfloat16), top_ref, kv_ref, q_all, p_ref, run_ref,
                do_ref, do_all, ds_all, dq_ref)
    own = own_rows_of(run_ref, block_ref[0] * BLOCK + lo, hi - lo)
    project_all(dq_ref[...], own, do_ref, wq, wkv, (send_ref, keep_ref, send2, keep2))


def early_top(
    block_ref, do_in, top_ref, kv_ref, q_all, p_ref, run_in, wq, wkv,
    send_ref, keep_ref, send2, keep2, carry_ref,
    dq_ref, do_ref, running, do_all, ds_all,
):
    lo, hi = HALVES[1]
    running[...] = run_in[...]
    early_terms(HALVES[1], do_in[...], top_ref, kv_ref, q_all, p_ref, running,
                do_ref, do_all, ds_all, dq_ref)
    first_row = block_ref[0] * BLOCK
    own = own_rows_of(running, first_row + lo, hi - lo)
    project_all(dq_ref[...], own, do_ref, wq, wkv, (send_ref, keep_ref, send2, keep2))
    below = lax.broadcasted_iota(jnp.int32, running.shape, 0) < first_row
    carry_ref[0] = jnp.where(below, running[...], 0.0).astype(jnp.bfloat16)


def finish(keep_t, got_t, keep_b, got_b, *refs):
    *pieces, out_ref = refs
    rows = pieces[0].shape[0]
    half = len(pieces) // 2
    for i, piece in enumerate(pieces):
        keep, got = (keep_t, got_t) if i < half else (keep_b, got_b)
        at = slice(i % half * rows, (i % half + 1) * rows)
        out_ref[0, i * rows : (i + 1) * rows] = total_of(keep[at], got[at], piece[...])


def add_rows(*refs):
    *ins, out_ref = refs
    out_ref[...] = total_of(*(ref[...] for ref in ins))


def add_halves(a_ref, b_ref, top_ref, bottom_ref):
    half = top_ref.shape[0]
    top_ref[...] = total_of(a_ref[:half], b_ref[:half])
    bottom_ref[...] = total_of(a_ref[half:], b_ref[half:])


SMEM = pl.BlockSpec(memory_space=pltpu.SMEM)
HBM = pl.BlockSpec(memory_space=pltpu.HBM)
VMEM = pl.BlockSpec(memory_space=pltpu.VMEM)


def call(kernel, name, specs, args, outs, scratch, megabytes):
    args = [
        pltpu.with_memory_space_constraint(arg, pltpu.HBM) if spec is HBM else arg
        for arg, spec in zip(args, specs)
    ]
    return pl.pallas_call(
        kernel,
        out_shape=[
            pltpu.HBM(*out[:2]) if len(out) > 2 else jax.ShapeDtypeStruct(*out) for out in outs
        ],
        in_specs=specs,
        out_specs=[HBM if len(out) > 2 else VMEM for out in outs],
        scratch_shapes=scratch,
        compiler_params=pltpu.CompilerParams(vmem_limit_bytes=megabytes * 1024 * 1024),
        cost_estimate=pl.CostEstimate(
            flops=2 * 10**9, bytes_accessed=10**6, transcendentals=0
        ),
        name=name,
    )(*args)


def add(name, *terms):
    shape = terms[0].shape
    (out,) = call(
        add_rows, name, [VMEM] * len(terms), terms, [(shape, jnp.bfloat16)], [], 4
    )
    return out


def swap(block, mask):
    return lax.ppermute(block, "tp", [(i, i ^ mask) for i in range(lax.axis_size("tp"))])


def shift_down(block, mask):
    sections, tp = lax.axis_size("section"), lax.axis_size("tp")
    route = [
        (s * tp + t, (s - 1) % sections * tp + (t ^ mask))
        for s in range(sections)
        for t in range(tp)
    ]
    return lax.ppermute(block, ("section", "tp"), route)


def total_of(*terms):
    out = terms[0].astype(jnp.float32)
    for term in terms[1:]:
        out = out + term.astype(jnp.float32)
    return out.astype(jnp.bfloat16)


def local(query, keyval, q_weight, kv_weight, block_index, carry_in, grad_late, grad_top):
    length = keyval.shape[1]
    half = BLOCK // 2
    tall_rows = BLOCK * WIDTH // HD
    bf16, f32 = jnp.bfloat16, jnp.float32
    block = ((BLOCK, WIDTH), bf16)
    half_block = ((half, WIDTH), bf16)
    half_tall = ((tall_rows // 2, HD), bf16)
    own_rows = ((BLOCK, KV_WIDTH), bf16)
    run_shape = ((length, KV_WIDTH), f32)
    kv_shape = ((length, KV_WIDTH), bf16)
    p_shapes = [((BLOCK + hi, tall_rows // 2), bf16) for _, hi in HALVES]
    q_load, kv_load = ((WIDTH, WIDTH), bf16), ((WIDTH, KV_WIDTH), bf16)
    several = lambda n, shape: ((n, *shape[0]), shape[1])
    send, keep, run, dq, own, wq, wkv = call(
        late_first,
        "late_first",
        [SMEM] + [HBM] * 6,
        [block_index, query, grad_late, keyval, carry_in, q_weight, kv_weight],
        [block, block, run_shape, block, own_rows]
        + [several(4, q_load), several(4, kv_load)],
        [
            pltpu.VMEM(*kv_shape),
            pltpu.VMEM(*kv_shape),
            pltpu.VMEM((tall_rows, HD), bf16),
            pltpu.VMEM((tall_rows, HD), bf16),
            pltpu.VMEM((length, tall_rows), bf16),
            pltpu.VMEM((length, tall_rows), bf16),
            pltpu.SemaphoreType.DMA((2,)),
            pltpu.SemaphoreType.DMA((2, WIDTH // HD)),
            pltpu.SemaphoreType.DMA((4, 2)),
        ],
        20,
    )
    got = swap(send, 1)
    send2, keep2 = call(
        late_second, "late_second", [VMEM] * 4, [dq, own, wq, wkv], [block] * 2, [], 8
    )
    got2 = swap(send2, 1)
    mine_t, mine_b = call(
        add_halves, "add_mine", [VMEM] * 2, [keep, got], [half_block] * 2, [], 4
    )
    straight = shift_down(mine_b, 0)
    other = swap(mine_t, 2)
    kept, crossed = call(
        add_halves, "add_crossed", [VMEM] * 2, [keep2, got2], [half_block, half_block], [], 4
    )
    crossed = shift_down(crossed, 2)
    p_b, p_t, q_b, q_t, kv_held, top_held = call(
        early_probabilities,
        "early_probabilities",
        [SMEM, HBM, HBM, HBM],
        [block_index, query, keyval, grad_top],
        [*p_shapes, half_tall, half_tall, kv_shape, block],
        [pltpu.SemaphoreType.DMA((2,)), pltpu.SemaphoreType.DMA((2, WIDTH // HD))],
        10,
    )
    kept, p_t = lax.optimization_barrier((kept, p_t))
    summed = shift_down(add("add_summed", kept, other), 2)
    half_scratch = [
        pltpu.VMEM(*half_block),
        pltpu.VMEM(*half_block),
        pltpu.VMEM(*half_tall),
        pltpu.VMEM(*p_shapes[0]),
    ]
    send_b, keep_b, send2_b, keep2_b, run = call(
        early_bottom,
        "early_bottom",
        [SMEM] + [VMEM] * 9,
        [block_index, straight, crossed, top_held, kv_held, q_b, p_b, run, wq, wkv],
        [half_block] * 4 + [run_shape],
        half_scratch,
        10,
    )
    got_b, got2_b = swap(send_b, 1), swap(send2_b, 1)
    send_t, keep_t, send2_t, keep2_t, carry = call(
        early_top,
        "early_top",
        [SMEM] + [VMEM] * 8,
        [block_index, summed, top_held, kv_held, q_t, p_t, run, wq, wkv],
        [half_block] * 4 + [((1, *kv_shape[0]), bf16)],
        half_scratch[:2] + [pltpu.VMEM(*run_shape)] + half_scratch[2:],
        10,
    )
    got_t, got2_t = swap(send_t, 1), swap(send2_t, 1)
    step = BLOCK // PIECES
    cuts = [slice(i * step, (i + 1) * step) for i in range(half // step)]
    from_b = [swap(total_of(keep_b[cut], got_b[cut]), 2) for cut in cuts]
    from_t = [swap(total_of(keep_t[cut], got_t[cut]), 2) for cut in cuts]
    (early_dx,) = call(
        finish,
        "finish",
        [VMEM] * (4 + PIECES),
        [keep2_t, got2_t, keep2_b, got2_b, *from_t, *from_b],
        [((1, BLOCK, WIDTH), bf16)],
        [],
        8,
    )
    return (early_dx, carry)


def solution(mesh):
    in_specs = (
        P("section", None, None, "tp"),
        P("section", None, "tp"),
        P("section", None, "tp"),
        P("section", None, "tp"),
        P("section"),
        P("section", None, "tp"),
        P("section", None, "tp"),
        P(None, "tp"),
    )
    out_specs = (P("section", None, "tp"), P("section", None, "tp"))
    return jax.shard_map(local, mesh=mesh, in_specs=in_specs, out_specs=out_specs, check_vma=False)
```
